128 devices in a mesh: row: 16 (over y, z_hi, core), col: 8 (over z_lo, x).
Axes of the slice: x: 4, y: 4, z: 4 (z_hi: 2, z_lo: 2; z = z_hi * 2 + z_lo), core: 2. Of those that a mesh axis runs over, the one named last changes fastest.
Arguments:
- features: bfloat16 [65536, 128], P(('row', 'col')), may hold values from -6 to 6
- weight: bfloat16 [128, 256], replicated, may hold values from -0.5 to 0.5
- layer_bias: float32 [256], replicated, may hold values from -1 to 1
- adj_tiles: bfloat16 [16, 8, 384, 128, 128], P('row', 'col'), may hold values from -0.109375 to 0.109375
- tile_rows: int32 [16, 8, 384], P('row', 'col'), may hold values from 0 to 31, as said below
- tile_cols: int32 [16, 8, 384], P('row', 'col'), may hold values from 0 to 63
- tile_counts: int32 [16, 8], P('row', 'col'), may hold values from 24 to 384, as said below
- cotangent: bfloat16 [65536, 256], P(('row', 'col')), may hold values from -30 to 30
Outputs:
- activated: bfloat16 [65536, 256], P(('row', 'col'))
- grad_features: bfloat16 [65536, 128], P(('row', 'col'))
- grad_weight: float32 [128, 256], replicated
- grad_bias: float32 [256], replicated
The draws below stay inside these ranges and needn't reach their ends.
Inputs may be any that keep to these rules, and one draw needn't show every extreme that they name: On each device the 384 pairs (tile_rows, tile_cols) of its slots are distinct. Slots from tile_counts on are ignored.
All inputs are finite; a program needn't handle non-finite values.
Results may differ from the reference program's by a relative error of at most 0.006.
Values may be sent and summed in bfloat16 or wider, within the bound.
No kernel may reach another device: no remote copies, remote signals or barrier semaphores. Data moves between devices by JAX's collectives and lax.ppermute only.
A program may use at most 128 MiB of HBM per device.

```python
import math
import jax
import jax.numpy as jnp
from jax import lax

F_IN = 128
F_OUT = 256
TILE = 128
SB = 4
TMAX = 384
RB = 32
CB = 64
NODES = 65536
N_ROW = 16
N_COL = 8


def tile_order(key):
    total = RB * CB
    shift_key, order_key = jax.random.split(key)
    device_keys = jax.random.split(order_key, N_ROW * N_COL)
    targets = jax.random.randint(shift_key, (N_ROW * N_COL,), 0, TMAX)

    def permute_one(device_key, target):
        shuffled = jax.random.permutation(device_key, total).astype(jnp.int32)
        where_last = jnp.argmax(shuffled == total - 1).astype(jnp.int32)
        return jnp.roll(shuffled, target - where_last)[:TMAX]
    return jax.vmap(permute_one)(device_keys, targets).reshape(N_ROW, N_COL, TMAX)


def draw_tile_rows(key, part):
    return tile_order(key) // CB


def draw_tile_cols(key, part):
    return tile_order(key) % CB


def draw_tile_counts(key, part):
    key = jax.random.fold_in(key, 5)
    first_key, second_key, third_key = jax.random.split(key, 3)
    first = jax.random.randint(first_key, (N_ROW * N_COL,), 1, TMAX + 1)
    second = jax.random.randint(second_key, (N_ROW * N_COL,), 1, TMAX + 1)
    counts = jnp.maximum(first * second // TMAX, max(TMAX // 16, 1))
    busiest = jax.random.randint(third_key, (), 0, N_ROW * N_COL)
    counts = jnp.where(jnp.arange(N_ROW * N_COL) == busiest, TMAX, counts)
    return counts.reshape(N_ROW, N_COL).astype(jnp.int32)


def draw_cotangent(key, part):
    key = jax.random.fold_in(key, 7)
    base_key, row_key, col_key = jax.random.split(key, 3)
    position = jnp.arange(NODES, dtype=jnp.float32)[:, None] / NODES
    base = jnp.clip(jax.random.normal(base_key, (NODES, F_OUT), jnp.float32), -6.0, 6.0)
    row_scale = jnp.exp(math.log(10.0) * (jax.random.uniform(row_key, (NODES, 1), jnp.float32) - 0.5))
    row_scale = row_scale * jnp.exp(math.log(3.0) * (position - 0.5))
    col_scale = jnp.exp(math.log(10.0) * (jax.random.uniform(col_key, (1, F_OUT), jnp.float32) - 0.5))
    return (0.25 * base * row_scale * col_scale).astype(jnp.bfloat16)


def block_levels(rng, extent, cuts, low, top_value):
    def one(dim, parts):
        heights = jax.random.uniform(jax.random.fold_in(jax.random.fold_in(rng, 6), dim), (parts,), jnp.float32, low / len(cuts), top_value / len(cuts))
        return jnp.repeat(jnp.exp(heights), extent[dim] // parts).reshape((-1,) + (1,) * (len(extent) - dim - 1))

    level = one(*cuts[0])
    for cut in cuts[1:]:
        level = level * one(*cut)
    return level


def centred(key, shape, spread, reach, pieces=(), kind=jnp.bfloat16):
    factor_of = block_levels(key, shape, pieces, -0.22, 0.18) if pieces else 1.0
    array = jax.random.normal(key, shape, jnp.float32) * spread * factor_of
    return jnp.minimum(jnp.maximum(array, -reach), reach).astype(kind)


def setup_inputs(seed: int = 0) -> dict:
    keys = jax.random.split(jax.random.key(seed), 9)
    features = centred(keys[0], (NODES, F_IN), 1.0, 6.0, ((0, 128),))
    weight = centred(keys[1], (F_IN, F_OUT), F_IN ** -0.5, 0.5)
    layer_bias = jnp.clip(jax.random.uniform(keys[2], (F_OUT,), jnp.float32, -1.0, 1.0), -1.0, 1.0)
    adj_tiles = centred(keys[3], (N_ROW, N_COL, TMAX, TILE, TILE), (TILE * TMAX // (4 * SB)) ** -0.5, 0.109375, ((0, 16), (1, 8)))
    tile_rows = draw_tile_rows(jax.random.fold_in(keys[8], 71), 0)
    tile_cols = draw_tile_cols(jax.random.fold_in(keys[8], 71), 0)
    tile_counts = draw_tile_counts(jax.random.fold_in(keys[8], 71), 0)
    cotangent = draw_cotangent(jax.random.fold_in(keys[8], 71), 0)
    return dict(features=features, weight=weight, layer_bias=layer_bias, adj_tiles=adj_tiles, tile_rows=tile_rows, tile_cols=tile_cols, tile_counts=tile_counts, cotangent=cotangent)


def device_product(tiles_dev, picks, places, live_count, source_blocks, out_blocks, flipped):
    slot_index = jnp.arange(TMAX, dtype=jnp.int32)
    living = (slot_index < live_count).astype(jnp.float32)
    sources = source_blocks[picks].astype(jnp.float32)
    pattern = 'tba,tbf->taf' if flipped else 'tab,tbf->taf'
    products = jnp.einsum(pattern, tiles_dev.astype(jnp.float32), sources) * living[:, None, None]
    return jax.ops.segment_sum(products, places, num_segments=out_blocks)

def reference(features, weight, layer_bias, adj_tiles, tile_rows, tile_cols, tile_counts, cotangent):
    layered = features.reshape(N_ROW, N_COL, SB * TILE, F_IN)
    col_groups = jnp.transpose(layered, (1, 0, 2, 3)).reshape(N_COL, CB, TILE, F_IN)

    def forward_row(row_index):

        def forward_device(col_index):
            return device_product(adj_tiles[row_index, col_index], tile_cols[row_index, col_index], tile_rows[row_index, col_index], tile_counts[row_index, col_index], col_groups[col_index], RB, False)
        return lax.optimization_barrier(jnp.sum(lax.map(forward_device, jnp.arange(N_COL, dtype=jnp.int32)), axis=0))
    aggregated = lax.map(forward_row, jnp.arange(N_ROW, dtype=jnp.int32)).reshape(NODES, F_IN)
    weight_wide = weight.astype(jnp.float32)
    summed = jnp.dot(aggregated, weight_wide, precision=lax.Precision.HIGHEST)
    squashed = jnp.tanh(summed + layer_bias)
    activated = squashed.astype(jnp.bfloat16)
    slopes = (cotangent.astype(jnp.float32) * (1.0 - squashed * squashed)).astype(jnp.bfloat16)
    row_groups = slopes.reshape(N_ROW, RB, TILE, F_OUT)

    def backward_col(col_index):

        def backward_device(row_index):
            return device_product(adj_tiles[row_index, col_index], tile_rows[row_index, col_index], tile_cols[row_index, col_index], tile_counts[row_index, col_index], row_groups[row_index], CB, True)
        return lax.optimization_barrier(jnp.sum(lax.map(backward_device, jnp.arange(N_ROW, dtype=jnp.int32)), axis=0))
    by_column = lax.map(backward_col, jnp.arange(N_COL, dtype=jnp.int32))
    node_grad = jnp.transpose(by_column.reshape(N_COL, N_ROW, SB * TILE, F_OUT), (1, 0, 2, 3)).reshape(NODES, F_OUT)
    grad_features = jnp.dot(node_grad, weight_wide.T, precision=lax.Precision.HIGHEST).astype(jnp.bfloat16)
    scaling = math.sqrt(NODES)
    slopes_wide = slopes.astype(jnp.float32)
    grad_weight = jnp.dot(aggregated.T, slopes_wide, precision=lax.Precision.HIGHEST) / scaling
    grad_bias = lax.optimization_barrier(jnp.sum(slopes_wide, axis=0)) / scaling
    return (activated, grad_features, grad_weight, grad_bias)
```

```python
import functools
import math

import jax
import jax.numpy as jnp
from jax import lax
from jax.experimental import pallas as pl
from jax.experimental.pallas import tpu as pltpu
from jax.sharding import PartitionSpec as P

f32 = jnp.float32
bf16 = jnp.bfloat16
STEP = 32
VMEM_BYTES = 44 << 20
SMEM_SPEC = pl.BlockSpec(memory_space=pltpu.SMEM)
VMEM_SPEC = pl.BlockSpec(memory_space=pltpu.VMEM)
ANY_SPEC = pl.BlockSpec(memory_space=pl.ANY)


def split(value):
    high = value.astype(bf16)
    return high, (value - high.astype(f32)).astype(bf16)


def tiles_kernel(flipped, starts, count_ref, place_ref, pick_ref, *refs):
    pieces = refs[: len(starts)]
    adj_ref, out_ref, total, tiles, source, tile_sem, piece_sem = refs[len(starts) :]
    out_blocks = out_ref.shape[0]
    size = adj_ref.shape[-1]
    count = count_ref[0]
    groups = (count + STEP - 1) // STEP

    def tile_copy(k):
        span = pl.ds(k * STEP, STEP)
        return pltpu.make_async_copy(adj_ref.at[span], tiles.at[span], tile_sem.at[k])

    def piece_copy(k):
        span = pl.ds(starts[k], pieces[k].shape[0])
        return pltpu.make_async_copy(pieces[k], source.at[span], piece_sem.at[k])

    for k in range(len(starts)):
        piece_copy(k).start()

    @pl.loop(0, groups)
    def _(k):
        tile_copy(k).start()

    @pl.loop(0, out_blocks + 1)
    def _(i):
        total[i] = jnp.zeros((size, size), f32)

    for k in range(len(starts)):
        piece_copy(k).wait()

    @pl.loop(0, groups)
    def _(k):
        tile_copy(k).wait()
        for u in range(STEP):
            slot = k * STEP + u
            place = jnp.where(slot < count, place_ref[slot], out_blocks)
            block = source[pick_ref[slot]]
            if flipped:
                product = jnp.dot(block, tiles[slot], preferred_element_type=f32)
            else:
                product = jnp.dot(tiles[slot], block, preferred_element_type=f32)
            total[place] += product

    @pl.loop(0, out_blocks // 4)
    def _(i):
        span = pl.ds(i * 4, 4)
        out_ref[span] = total[span].astype(out_ref.dtype)


def tile_products(count, place, pick, pieces, adj, out_blocks, flipped):
    slots, size, _ = adj.shape
    starts, filled = [], 0
    for piece in pieces:
        starts.append(filled)
        filled += piece.shape[0]
    return pl.pallas_call(
        functools.partial(tiles_kernel, flipped, tuple(starts)),
        out_shape=jax.ShapeDtypeStruct((out_blocks, size, size), bf16),
        in_specs=[SMEM_SPEC] * 3 + [ANY_SPEC] * (len(pieces) + 1),
        out_specs=VMEM_SPEC,
        scratch_shapes=[
            pltpu.VMEM((out_blocks + 1, size, size), f32),
            pltpu.VMEM((slots, size, size), bf16),
            pltpu.VMEM((filled, size, size), bf16),
            pltpu.SemaphoreType.DMA((slots // STEP,)),
            pltpu.SemaphoreType.DMA((len(pieces),)),
        ],
        compiler_params=pltpu.CompilerParams(vmem_limit_bytes=VMEM_BYTES),
        name="backward_tiles" if flipped else "forward_tiles",
    )(count, place, pick, *pieces, adj)


def layer_kernel(parts_ref, weight_ref, bias_ref, cot_ref, act_ref, turned_ref, grads_ref):
    aggregated = jnp.sum(parts_ref[...].astype(f32), axis=0)
    weight = weight_ref[...]
    high, low = split(aggregated)
    summed = jnp.dot(high, weight, preferred_element_type=f32)
    summed += jnp.dot(low, weight, preferred_element_type=f32)
    squashed = jnp.tanh(summed + bias_ref[...])
    act_ref[...] = squashed.astype(bf16)
    slopes = (cot_ref[...].astype(f32) * (1.0 - squashed * squashed)).astype(bf16)
    size = turned_ref.shape[-1]
    for i in range(turned_ref.shape[0]):
        rows = slopes[i * size : (i + 1) * size]
        turned_ref[i] = lax.dot_general(
            weight, rows, (((1,), (1,)), ((), ())), preferred_element_type=f32
        ).astype(bf16)
    high_t, low_t = split(aggregated.T)
    term = jnp.dot(high_t, slopes, preferred_element_type=f32)
    term += jnp.dot(low_t, slopes, preferred_element_type=f32)
    width = slopes.shape[1]
    grads_ref[:, :width] = term
    bias_term = jnp.sum(slopes.astype(f32), axis=0, keepdims=True)
    grads_ref[:, width:] = jnp.broadcast_to(bias_term, term.shape)


def layer(parts, weight, bias, cotangent):
    nodes, units = cotangent.shape
    features = weight.shape[0]
    return pl.pallas_call(
        layer_kernel,
        out_shape=(
            jax.ShapeDtypeStruct((nodes, units), bf16),
            jax.ShapeDtypeStruct((nodes // 128, features, 128), bf16),
            jax.ShapeDtypeStruct((features, 2 * units), f32),
        ),
        in_specs=[VMEM_SPEC] * 4,
        out_specs=(VMEM_SPEC,) * 3,
        compiler_params=pltpu.CompilerParams(vmem_limit_bytes=VMEM_BYTES),
        name="layer",
    )(parts, weight, bias.reshape(1, units), cotangent)


def turn_kernel(parts_ref, out_ref):
    size = parts_ref.shape[-1]
    for i in range(parts_ref.shape[1]):
        total = jnp.sum(parts_ref[:, i].astype(f32), axis=0)
        out_ref[i * size : (i + 1) * size, :] = total.T.astype(bf16)


def turn(parts):
    _, blocks, features, size = parts.shape
    return pl.pallas_call(
        turn_kernel,
        out_shape=jax.ShapeDtypeStruct((blocks * size, features), bf16),
        in_specs=[VMEM_SPEC],
        out_specs=VMEM_SPEC,
        compiler_params=pltpu.CompilerParams(vmem_limit_bytes=VMEM_BYTES),
        name="turn",
    )(parts)


def on_device(
    features, weight, layer_bias, adj_tiles, tile_rows, tile_cols, tile_counts, cotangent
):
    row_count = lax.axis_size("row")
    col_count = lax.axis_size("col")
    size = adj_tiles.shape[-1]
    own = features.shape[0] // size
    row_blocks = own * col_count
    col_blocks = own * row_count
    half = row_count // 2
    node_total = features.shape[0] * row_count * col_count
    adj = adj_tiles[0, 0]
    rows = tile_rows[0, 0]
    cols = tile_cols[0, 0]
    count = tile_counts[0]
    my_row = lax.axis_index("row")
    my_col = lax.axis_index("col")
    cores = [[2 * k + c for k in range(half)] for c in range(2)]
    sibling = [(i, i ^ 1) for i in range(row_count)]

    mine = features.reshape(1, own, size, -1)
    mine = lax.all_to_all(
        jnp.broadcast_to(mine, (half,) + mine.shape[1:]),
        "row", 0, 0, tiled=True, axis_index_groups=cores,
    ).reshape(half * own, size, -1)
    other = lax.ppermute(mine, "row", sibling)
    owner = cols // own
    cols_slot = ((owner ^ my_row) & 1) * (half * own) + (owner // 2) * own + cols % own
    partial_value = tile_products(count, rows, cols_slot, [mine, other], adj, row_blocks, False)
    parts = lax.all_to_all(
        partial_value.reshape(col_count, own * size, -1), "col", 0, 0, tiled=True
    )
    activated, turned, grads = layer(parts, weight, layer_bias, cotangent)

    pair = lax.ppermute(turned, "col", [(i, i ^ 4) for i in range(col_count)])
    up = [(i, (i // 4) * 4 + (i + 1) % 4) for i in range(col_count)]
    down = [(i, (i // 4) * 4 + (i + 3) % 4) for i in range(col_count)]
    pieces = []
    for block in (turned, pair):
        before = lax.ppermute(block, "col", up)
        after = lax.ppermute(block, "col", down)
        far_top = lax.ppermute(before[: own // 2], "col", up)
        far_low = lax.ppermute(after[own // 2 :], "col", down)
        pieces += [block, after, far_top, far_low, before]
    owner = rows // own
    far = ((owner ^ my_col) // 4) * 4 + (owner - my_col) % 4
    rows_slot = far * own + rows % own
    partial_grad = tile_products(count, cols_slot, rows_slot, pieces, adj, col_blocks, True)
    mine, other = partial_grad[: half * own], partial_grad[half * own :]
    other = lax.ppermute(other, "row", sibling)
    both = (mine.astype(f32) + other.astype(f32)).astype(bf16)
    both = lax.all_to_all(
        both.reshape(half, own, size, size), "row", 0, 0, tiled=True, axis_index_groups=cores
    )
    grad_features = turn(both)

    scaling = math.sqrt(node_total)
    units = weight.shape[1]
    everywhere = ("row", "col")
    mixed = lax.all_to_all(grads, everywhere, 0, 0, tiled=True)
    sums = jnp.sum(mixed, axis=0, keepdims=True) / scaling
    grad_weight = lax.all_to_all(
        jnp.broadcast_to(sums[:, :units], (weight.shape[0], units)), everywhere, 0, 0, tiled=True
    )
    return activated, grad_features, grad_weight, sums[0, units:]


def solution(mesh):
    placed = (
        P(("row", "col"), None),
        P(),
        P(),
        P("row", "col", None, None, None),
        P("row", "col", None),
        P("row", "col", None),
        P("row", "col"),
        P(("row", "col"), None),
    )
    return jax.shard_map(
        on_device,
        mesh=mesh,
        in_specs=placed,
        out_specs=(P(("row", "col"), None), P(("row", "col"), None), P(), P()),
        check_vma=False,
    )
```

```python
import functools
import math

import jax
import jax.numpy as jnp
from jax import lax
from jax.experimental import pallas as pl
from jax.experimental.pallas import tpu as pltpu
from jax.sharding import PartitionSpec as P

f32 = jnp.float32
bf16 = jnp.bfloat16
STEP = 32
BIAS_ROWS = 8
VMEM_BYTES = 44 << 20
SMEM_SPEC = pl.BlockSpec(memory_space=pltpu.SMEM)
VMEM_SPEC = pl.BlockSpec(memory_space=pltpu.VMEM)
ANY_SPEC = pl.BlockSpec(memory_space=pl.ANY)


def nearness(chip, me):
    return ((chip ^ me) % 2) * 4 + (chip // 2 + 4 - me // 2) % 4


def split(value):
    high = value.astype(bf16)
    return high, (value - high.astype(f32)).astype(bf16)


def tiles_kernel(flipped, starts, waits, count_ref, place_ref, pick_ref, *refs):
    pieces = refs[: len(starts)]
    refs = refs[len(starts) + waits :]
    adj_ref, *outs, total, tiles, source, tile_sem, piece_sem = refs
    out_blocks = sum(out.shape[0] for out in outs)
    size = adj_ref.shape[-1]
    count = count_ref[0]
    groups = (count + STEP - 1) // STEP

    def tile_copy(k):
        span = pl.ds(k * STEP, STEP)
        return pltpu.make_async_copy(adj_ref.at[span], tiles.at[span], tile_sem.at[k])

    def piece_copy(k):
        span = pl.ds(starts[k], pieces[k].shape[0])
        return pltpu.make_async_copy(pieces[k], source.at[span], piece_sem.at[k])

    for k in range(len(starts)):
        piece_copy(k).start()

    @pl.loop(0, groups)
    def _(k):
        tile_copy(k).start()

    @pl.loop(0, out_blocks + 1)
    def _(i):
        total[i] = jnp.zeros((size, size), f32)

    for k in range(len(starts)):
        piece_copy(k).wait()

    @pl.loop(0, groups)
    def _(k):
        tile_copy(k).wait()
        for u in range(STEP):
            slot = k * STEP + u
            place = jnp.where(slot < count, place_ref[slot], out_blocks)
            block = source[pick_ref[slot]]
            if flipped:
                product = jnp.dot(block, tiles[slot], preferred_element_type=f32)
            else:
                product = jnp.dot(tiles[slot], block, preferred_element_type=f32)
            total[place] += product

    filled = 0
    for out in outs:

        @pl.loop(0, out.shape[0] // 4)
        def _(i, out=out, filled=filled):
            out[pl.ds(i * 4, 4)] = total[pl.ds(filled + i * 4, 4)].astype(out.dtype)

        filled += out.shape[0]


def tile_products(count, place, pick, pieces, adj, outs, flipped, after=()):
    out_blocks = sum(outs)
    slots, size, _ = adj.shape
    starts, filled = [], 0
    for piece in pieces:
        starts.append(filled)
        filled += piece.shape[0]
    cost = pl.CostEstimate(
        flops=2 * slots * size**3, bytes_accessed=2 * slots * size**2, transcendentals=0
    )
    return pl.pallas_call(
        functools.partial(tiles_kernel, flipped, tuple(starts), len(after)),
        cost_estimate=cost,
        out_shape=tuple(jax.ShapeDtypeStruct((n, size, size), bf16) for n in outs),
        in_specs=[SMEM_SPEC] * 3 + [ANY_SPEC] * (len(pieces) + len(after) + 1),
        out_specs=(VMEM_SPEC,) * len(outs),
        scratch_shapes=[
            pltpu.VMEM((out_blocks + 1, size, size), f32),
            pltpu.VMEM((slots, size, size), bf16),
            pltpu.VMEM((filled, size, size), bf16),
            pltpu.SemaphoreType.DMA((slots // STEP,)),
            pltpu.SemaphoreType.DMA((len(pieces),)),
        ],
        compiler_params=pltpu.CompilerParams(vmem_limit_bytes=VMEM_BYTES),
        name="backward_tiles" if flipped else "forward_tiles",
    )(count, place, pick, *pieces, *after, adj)


def layer_kernel(me_ref, parts_ref, weight_ref, bias_ref, cot_ref, act_ref, turned_ref, grads_ref):
    aggregated = jnp.sum(parts_ref[...].astype(f32), axis=0)
    weight = weight_ref[...]
    high, low = split(aggregated)
    summed = jnp.dot(high, weight, preferred_element_type=f32)
    summed += jnp.dot(low, weight, preferred_element_type=f32)
    squashed = jnp.tanh(summed + bias_ref[...])
    act_ref[...] = squashed.astype(bf16)
    slopes = (cot_ref[...].astype(f32) * (1.0 - squashed * squashed)).astype(bf16)
    size = turned_ref.shape[-1]
    for i in range(turned_ref.shape[0]):
        rows = slopes[i * size : (i + 1) * size]
        turned_ref[i] = lax.dot_general(
            weight, rows, (((1,), (1,)), ((), ())), preferred_element_type=f32
        ).astype(bf16)
    high_t, low_t = split(aggregated.T)
    term = jnp.dot(high_t, slopes, preferred_element_type=f32)
    term += jnp.dot(low_t, slopes, preferred_element_type=f32)
    bias_term = jnp.sum(slopes.astype(f32), axis=0, keepdims=True)
    chunks, rows, width = grads_ref.shape
    held = rows - BIAS_ROWS
    for chunk in range(chunks):
        place = nearness(chunk, me_ref[0])
        grads_ref[place, :held] = term[chunk * held : (chunk + 1) * held]
        grads_ref[place, held:] = jnp.broadcast_to(bias_term, (BIAS_ROWS, width))


def layer(me, parts, weight, bias, cotangent, chips):
    nodes, units = cotangent.shape
    features = weight.shape[0]
    return pl.pallas_call(
        layer_kernel,
        out_shape=(
            jax.ShapeDtypeStruct((nodes, units), bf16),
            jax.ShapeDtypeStruct((nodes // 128, features, 128), bf16),
            jax.ShapeDtypeStruct((chips, features // chips + BIAS_ROWS, units), f32),
        ),
        in_specs=[SMEM_SPEC] + [VMEM_SPEC] * 4,
        out_specs=(VMEM_SPEC,) * 3,
        compiler_params=pltpu.CompilerParams(vmem_limit_bytes=VMEM_BYTES),
        name="layer",
    )(me, parts, weight, bias.reshape(1, units), cotangent)


def join_kernel(scale, mine_ref, other_ref, near_ref, far_ref, up_ref, down_ref, out_ref, bias_ref):
    pieces, blocks, size, _ = mine_ref.shape
    total = ((near_ref[0] + far_ref[0]) + (up_ref[0] + down_ref[0])) * scale
    held = total.shape[0] - BIAS_ROWS
    bias_ref[...] = total[held:]
    high, low = split(total[:held])
    extra = jnp.concatenate([high[:, :size], high[:, size:], low[:, :size], low[:, size:]], axis=0)

    @pl.loop(0, pieces)
    def _(i):
        for b in range(blocks):
            both = mine_ref[i, b].astype(f32) + other_ref[i, b].astype(f32)
            out_ref[i, b * size : (b + 1) * size] = both.astype(bf16)
        out_ref[i, blocks * size :] = extra


def join(scale, mine, other, terms):
    pieces, blocks, size, _ = mine.shape
    _, rows, units = terms[0].shape
    extra = 2 * (rows - BIAS_ROWS) * units // size
    return pl.pallas_call(
        functools.partial(join_kernel, scale),
        out_shape=(
            jax.ShapeDtypeStruct((pieces, blocks * size + extra, size), bf16),
            jax.ShapeDtypeStruct((BIAS_ROWS, units), f32),
        ),
        in_specs=[VMEM_SPEC] * 6,
        out_specs=(VMEM_SPEC,) * 2,
        compiler_params=pltpu.CompilerParams(vmem_limit_bytes=VMEM_BYTES),
        name="join",
    )(mine, other, *terms)


def turn_kernel(parts_ref, out_ref, grad_ref):
    pieces, rows, size = parts_ref.shape
    blocks = out_ref.shape[0] // size
    for i in range(blocks):
        total = jnp.sum(parts_ref[:, i * size : (i + 1) * size].astype(f32), axis=0)
        out_ref[i * size : (i + 1) * size, :] = total.T.astype(bf16)
    quarter = (rows - blocks * size) // 4
    for p in range(pieces):
        part = [
            parts_ref[p, blocks * size + q * quarter : blocks * size + (q + 1) * quarter].astype(f32)
            for q in range(4)
        ]
        span = slice(p * quarter, (p + 1) * quarter)
        grad_ref[span, :size] = part[0] + part[2]
        grad_ref[span, size:] = part[1] + part[3]


def turn(parts, blocks, weight):
    size = parts.shape[-1]
    return pl.pallas_call(
        turn_kernel,
        out_shape=(
            jax.ShapeDtypeStruct((blocks * size, size), bf16),
            jax.ShapeDtypeStruct(weight.shape, f32),
        ),
        in_specs=[VMEM_SPEC],
        out_specs=(VMEM_SPEC,) * 2,
        compiler_params=pltpu.CompilerParams(vmem_limit_bytes=VMEM_BYTES),
        name="turn",
    )(parts)


def on_device(
    features, weight, layer_bias, adj_tiles, tile_rows, tile_cols, tile_counts, cotangent
):
    row_count = lax.axis_size("row")
    col_count = lax.axis_size("col")
    size = adj_tiles.shape[-1]
    own = features.shape[0] // size
    row_blocks = own * col_count
    col_blocks = own * row_count
    half = row_count // 2
    node_total = features.shape[0] * row_count * col_count
    adj = adj_tiles[0, 0]
    rows = tile_rows[0, 0]
    cols = tile_cols[0, 0]
    count = tile_counts[0]
    my_row = lax.axis_index("row")
    my_col = lax.axis_index("col")
    chip = (my_row // 2).reshape(1)
    cores = [[2 * k + c for k in range(half)] for c in range(2)]
    sibling = [(i, i ^ 1) for i in range(row_count)]

    mine = features.reshape(1, own, size, -1)
    mine = lax.all_to_all(
        jnp.broadcast_to(mine, (half,) + mine.shape[1:]),
        "row", 0, 0, tiled=True, axis_index_groups=cores,
    ).reshape(half * own, size, -1)
    other = lax.ppermute(mine, "row", sibling)
    owner = cols // own
    cols_slot = ((owner ^ my_row) & 1) * (half * own) + (owner // 2) * own + cols % own
    (partial_value,) = tile_products(count, rows, cols_slot, [mine, other], adj, [row_blocks], False)
    parts = lax.all_to_all(
        partial_value.reshape(col_count, own * size, -1), "col", 0, 0, tiled=True
    )
    activated, turned, grads = layer(chip, parts, weight, layer_bias, cotangent, half)

    pair = lax.ppermute(turned, "col", [(i, i ^ 4) for i in range(col_count)])
    up = [(i, (i // 4) * 4 + (i + 1) % 4) for i in range(col_count)]
    down = [(i, (i // 4) * 4 + (i + 3) % 4) for i in range(col_count)]
    block = jnp.concatenate([turned, pair], axis=0)
    before = lax.ppermute(block, "col", up)
    after = lax.ppermute(block, "col", down)
    far_top = lax.ppermute(before[:own], "col", up)
    far_low = lax.ppermute(after[own:], "col", down)
    pieces = [block, after, far_top, far_low, before]
    owner = rows // own
    far = ((owner - my_col) % 4) * 2 + (owner ^ my_col) // 4
    rows_slot = far * own + rows % own
    grads += lax.ppermute(grads, "row", sibling)
    grads = grads[:4] + lax.ppermute(grads[4:], "row", [(i, i ^ 2) for i in range(row_count)])
    y_up = [(i, (i + 4) % row_count) for i in range(row_count)]
    y_down = [(i, (i - 4) % row_count) for i in range(row_count)]
    y_far = [(i, (i + 8) % row_count) for i in range(row_count)]
    grads = (grads[:1] + lax.ppermute(grads[2:3], "row", y_far)) + (
        lax.ppermute(grads[1:2], "row", y_up) + lax.ppermute(grads[3:4], "row", y_down)
    )
    row_sums = grads
    grads += lax.ppermute(grads, "col", [(i, i ^ 4) for i in range(col_count)])
    x_far = [(i, (i // 4) * 4 + (i + 2) % 4) for i in range(col_count)]
    terms = [grads] + [lax.ppermute(grads, "col", to) for to in (x_far, up, down)]

    mine, other = tile_products(count, cols_slot, rows_slot, pieces, adj, [col_blocks // 2] * 2, True, [row_sums])
    other = lax.ppermute(other, "row", sibling)
    piece = (half, own, size, size)
    both, bias_sums = join(
        1.0 / math.sqrt(node_total), mine.reshape(piece), other.reshape(piece), terms
    )
    both = lax.all_to_all(both, "row", 0, 0, tiled=True, axis_index_groups=cores)
    grad_features, grad_weight = turn(both, own, weight)
    return activated, grad_features, grad_weight, bias_sums[0]


def solution(mesh):
    placed = (
        P(("row", "col"), None),
        P(),
        P(),
        P("row", "col", None, None, None),
        P("row", "col", None),
        P("row", "col", None),
        P("row", "col"),
        P(("row", "col"), None),
    )
    return jax.shard_map(
        on_device,
        mesh=mesh,
        in_specs=placed,
        out_specs=(P(("row", "col"), None), P(("row", "col"), None), P(), P()),
        check_vma=False,
    )
```

```python
import functools
import math

import jax
import jax.numpy as jnp
from jax import lax
from jax.experimental import pallas as pl
from jax.experimental.pallas import tpu as pltpu
from jax.sharding import PartitionSpec as P

f32 = jnp.float32
bf16 = jnp.bfloat16
STEP = 32
BIAS_ROWS = 8
VMEM_BYTES = 44 << 20
SMEM_SPEC = pl.BlockSpec(memory_space=pltpu.SMEM)
VMEM_SPEC = pl.BlockSpec(memory_space=pltpu.VMEM)
ANY_SPEC = pl.BlockSpec(memory_space=pl.ANY)


def nearness(chip, me):
    return (chip // 2 + 4 - me // 2) % 4 * 2 + (chip ^ me) % 2


def split(value):
    high = value.astype(bf16)
    return high, (value - high.astype(f32)).astype(bf16)


def tiles_kernel(flipped, starts, waits, count_ref, place_ref, pick_ref, *refs):
    pieces = refs[: len(starts)]
    refs = refs[len(starts) + waits :]
    adj_ref, *outs, total, tiles, source, tile_sem, piece_sem = refs
    out_blocks = sum(out.shape[0] for out in outs)
    size = adj_ref.shape[-1]
    count = count_ref[0]
    groups = (count + STEP - 1) // STEP

    def tile_copy(k):
        span = pl.ds(k * STEP, STEP)
        return pltpu.make_async_copy(adj_ref.at[span], tiles.at[span], tile_sem.at[k])

    def piece_copy(k):
        span = pl.ds(starts[k], pieces[k].shape[0])
        return pltpu.make_async_copy(pieces[k], source.at[span], piece_sem.at[k])

    for k in range(len(starts)):
        piece_copy(k).start()

    @pl.loop(0, groups)
    def _(k):
        tile_copy(k).start()

    @pl.loop(0, out_blocks + 1)
    def _(i):
        total[i] = jnp.zeros((size, size), f32)

    for k in range(len(starts)):
        piece_copy(k).wait()

    @pl.loop(0, groups)
    def _(k):
        tile_copy(k).wait()
        for u in range(STEP):
            slot = k * STEP + u
            place = jnp.where(slot < count, place_ref[slot], out_blocks)
            block = source[pick_ref[slot]]
            if flipped:
                product = jnp.dot(block, tiles[slot], preferred_element_type=f32)
            else:
                product = jnp.dot(tiles[slot], block, preferred_element_type=f32)
            total[place] += product

    filled = 0
    for out in outs:

        @pl.loop(0, out.shape[0] // 4)
        def _(i, out=out, filled=filled):
            out[pl.ds(i * 4, 4)] = total[pl.ds(filled + i * 4, 4)].astype(out.dtype)

        filled += out.shape[0]


def tile_products(count, place, pick, pieces, adj, outs, flipped, after=()):
    out_blocks = sum(outs)
    slots, size, _ = adj.shape
    starts, filled = [], 0
    for piece in pieces:
        starts.append(filled)
        filled += piece.shape[0]
    cost = pl.CostEstimate(
        flops=2 * slots * size**3, bytes_accessed=2 * slots * size**2, transcendentals=0
    )
    return pl.pallas_call(
        functools.partial(tiles_kernel, flipped, tuple(starts), len(after)),
        cost_estimate=cost,
        out_shape=tuple(jax.ShapeDtypeStruct((n, size, size), bf16) for n in outs),
        in_specs=[SMEM_SPEC] * 3 + [ANY_SPEC] * (len(pieces) + len(after) + 1),
        out_specs=(VMEM_SPEC,) * len(outs),
        scratch_shapes=[
            pltpu.VMEM((out_blocks + 1, size, size), f32),
            pltpu.VMEM((slots, size, size), bf16),
            pltpu.VMEM((filled, size, size), bf16),
            pltpu.SemaphoreType.DMA((slots // STEP,)),
            pltpu.SemaphoreType.DMA((len(pieces),)),
        ],
        compiler_params=pltpu.CompilerParams(vmem_limit_bytes=VMEM_BYTES),
        name="backward_tiles" if flipped else "forward_tiles",
    )(count, place, pick, *pieces, *after, adj)


def layer_kernel(me_ref, parts_ref, weight_ref, bias_ref, cot_ref, act_ref, turned_ref, grads_ref):
    aggregated = jnp.sum(parts_ref[...].astype(f32), axis=0)
    weight = weight_ref[...]
    high, low = split(aggregated)
    summed = jnp.dot(high, weight, preferred_element_type=f32)
    summed += jnp.dot(low, weight, preferred_element_type=f32)
    squashed = jnp.tanh(summed + bias_ref[...])
    act_ref[...] = squashed.astype(bf16)
    slopes = (cot_ref[...].astype(f32) * (1.0 - squashed * squashed)).astype(bf16)
    size = turned_ref.shape[-1]
    for i in range(turned_ref.shape[0]):
        rows = slopes[i * size : (i + 1) * size]
        turned_ref[i] = lax.dot_general(
            weight, rows, (((1,), (1,)), ((), ())), preferred_element_type=f32
        ).astype(bf16)
    high_t, low_t = split(aggregated.T)
    term = jnp.dot(high_t, slopes, preferred_element_type=f32)
    term += jnp.dot(low_t, slopes, preferred_element_type=f32)
    bias_term = jnp.sum(slopes.astype(f32), axis=0, keepdims=True)
    chunks, rows, width = grads_ref.shape
    held = rows - BIAS_ROWS
    for chunk in range(chunks):
        place = nearness(chunk, me_ref[0])
        grads_ref[place, :held] = term[chunk * held : (chunk + 1) * held]
        grads_ref[place, held:] = jnp.broadcast_to(bias_term, (BIAS_ROWS, width))


def layer(me, parts, weight, bias, cotangent, chips):
    nodes, units = cotangent.shape
    features = weight.shape[0]
    return pl.pallas_call(
        layer_kernel,
        out_shape=(
            jax.ShapeDtypeStruct((nodes, units), bf16),
            jax.ShapeDtypeStruct((nodes // 128, features, 128), bf16),
            jax.ShapeDtypeStruct((chips, features // chips + BIAS_ROWS, units), f32),
        ),
        in_specs=[SMEM_SPEC] + [VMEM_SPEC] * 4,
        out_specs=(VMEM_SPEC,) * 3,
        compiler_params=pltpu.CompilerParams(vmem_limit_bytes=VMEM_BYTES),
        name="layer",
    )(me, parts, weight, bias.reshape(1, units), cotangent)


def ring_sum_kernel(passing, *refs):
    own_ref, far_ref, up_ref, down_ref = refs[passing : passing + 4]
    kept = far_ref.shape[0]
    out_ref = refs[-1]
    out_ref[...] = (own_ref[:kept] + far_ref[...]) + (up_ref[...] + down_ref[...])


def ring_sum(passing, terms):
    count = len(passing)
    return pl.pallas_call(
        functools.partial(ring_sum_kernel, count),
        out_shape=tuple(jax.ShapeDtypeStruct(x.shape, x.dtype) for x in passing)
        + (jax.ShapeDtypeStruct(terms[1].shape, f32),),
        in_specs=[VMEM_SPEC] * count + [VMEM_SPEC] * 4,
        out_specs=(VMEM_SPEC,) * count + (VMEM_SPEC,),
        input_output_aliases={i: i for i in range(count)},
        compiler_params=pltpu.CompilerParams(vmem_limit_bytes=16 << 20),
        name="ring_sum",
    )(*passing, *terms)


def join_kernel(scale, mine_ref, other_ref, near_ref, far_ref, out_ref, bias_ref):
    pieces, blocks, size, _ = mine_ref.shape
    total = (near_ref[0] + far_ref[0]) * scale
    held = total.shape[0] - BIAS_ROWS
    bias_ref[...] = total[held:]
    high, low = split(total[:held])
    extra = jnp.concatenate([high[:, :size], high[:, size:], low[:, :size], low[:, size:]], axis=0)

    @pl.loop(0, pieces)
    def _(i):
        for b in range(blocks):
            both = mine_ref[i, b].astype(f32) + other_ref[i, b].astype(f32)
            out_ref[i, b * size : (b + 1) * size] = both.astype(bf16)
        out_ref[i, blocks * size :] = extra


def join(scale, mine, other, terms):
    pieces, blocks, size, _ = mine.shape
    _, rows, units = terms[0].shape
    extra = 2 * (rows - BIAS_ROWS) * units // size
    return pl.pallas_call(
        functools.partial(join_kernel, scale),
        out_shape=(
            jax.ShapeDtypeStruct((pieces, blocks * size + extra, size), bf16),
            jax.ShapeDtypeStruct((BIAS_ROWS, units), f32),
        ),
        in_specs=[VMEM_SPEC] * 4,
        out_specs=(VMEM_SPEC,) * 2,
        compiler_params=pltpu.CompilerParams(vmem_limit_bytes=VMEM_BYTES),
        name="join",
    )(mine, other, *terms)


def turn_kernel(parts_ref, out_ref, grad_ref):
    pieces, rows, size = parts_ref.shape
    blocks = out_ref.shape[0] // size
    for i in range(blocks):
        total = jnp.sum(parts_ref[:, i * size : (i + 1) * size].astype(f32), axis=0)
        out_ref[i * size : (i + 1) * size, :] = total.T.astype(bf16)
    quarter = (rows - blocks * size) // 4
    for p in range(pieces):
        part = [
            parts_ref[p, blocks * size + q * quarter : blocks * size + (q + 1) * quarter].astype(f32)
            for q in range(4)
        ]
        span = slice(p * quarter, (p + 1) * quarter)
        grad_ref[span, :size] = part[0] + part[2]
        grad_ref[span, size:] = part[1] + part[3]


def turn(parts, blocks, weight):
    size = parts.shape[-1]
    return pl.pallas_call(
        turn_kernel,
        out_shape=(
            jax.ShapeDtypeStruct((blocks * size, size), bf16),
            jax.ShapeDtypeStruct(weight.shape, f32),
        ),
        in_specs=[VMEM_SPEC],
        out_specs=(VMEM_SPEC,) * 2,
        compiler_params=pltpu.CompilerParams(vmem_limit_bytes=VMEM_BYTES),
        name="turn",
    )(parts)


def on_device(
    features, weight, layer_bias, adj_tiles, tile_rows, tile_cols, tile_counts, cotangent
):
    row_count = lax.axis_size("row")
    col_count = lax.axis_size("col")
    size = adj_tiles.shape[-1]
    own = features.shape[0] // size
    row_blocks = own * col_count
    col_blocks = own * row_count
    half = row_count // 2
    node_total = features.shape[0] * row_count * col_count
    adj = adj_tiles[0, 0]
    rows = tile_rows[0, 0]
    cols = tile_cols[0, 0]
    count = tile_counts[0]
    my_row = lax.axis_index("row")
    my_col = lax.axis_index("col")
    chip = (my_row // 2).reshape(1)
    cores = [[2 * k + c for k in range(half)] for c in range(2)]
    sibling = [(i, i ^ 1) for i in range(row_count)]

    mine = features.reshape(1, own, size, -1)
    mine = lax.all_to_all(
        jnp.broadcast_to(mine, (half,) + mine.shape[1:]),
        "row", 0, 0, tiled=True, axis_index_groups=cores,
    ).reshape(half * own, size, -1)
    other = lax.ppermute(mine, "row", sibling)
    owner = cols // own
    cols_slot = ((owner ^ my_row) & 1) * (half * own) + (owner // 2) * own + cols % own
    (partial_value,) = tile_products(count, rows, cols_slot, [mine, other], adj, [row_blocks], False)
    parts = lax.all_to_all(
        partial_value.reshape(col_count, own * size, -1), "col", 0, 0, tiled=True
    )
    activated, turned, grads = layer(chip, parts, weight, layer_bias, cotangent, half)

    pair = lax.ppermute(turned, "col", [(i, i ^ 4) for i in range(col_count)])
    up = [(i, (i // 4) * 4 + (i + 1) % 4) for i in range(col_count)]
    down = [(i, (i // 4) * 4 + (i + 3) % 4) for i in range(col_count)]
    block = jnp.concatenate([turned, pair], axis=0)
    before = lax.ppermute(block, "col", up)
    after = lax.ppermute(block, "col", down)
    far_top = lax.ppermute(before[:own], "col", up)
    far_low = lax.ppermute(after[own:], "col", down)
    pieces = [block, after, far_top, far_low, before]
    owner = rows // own
    far = ((owner - my_col) % 4) * 2 + (owner ^ my_col) // 4
    rows_slot = far * own + rows % own
    grads += lax.ppermute(grads, "row", sibling)
    y_up = [(i, (i + 4) % row_count) for i in range(row_count)]
    y_down = [(i, (i - 4) % row_count) for i in range(row_count)]
    y_far = [(i, (i + 8) % row_count) for i in range(row_count)]
    grads = (grads[:2] + lax.ppermute(grads[4:6], "row", y_far)) + (
        lax.ppermute(grads[2:4], "row", y_up) + lax.ppermute(grads[6:], "row", y_down)
    )
    row_sums = grads[:1] + lax.ppermute(grads[1:], "row", [(i, i ^ 2) for i in range(row_count)])
    x_far = [(i, (i // 4) * 4 + (i + 2) % 4) for i in range(col_count)]
    terms = [row_sums] + [lax.ppermute(row_sums, "col", to) for to in (x_far, up, down)]

    mine, other = tile_products(count, cols_slot, rows_slot, pieces, adj, [col_blocks // 2] * 2, True, [row_sums])
    other, col_sums = ring_sum([other], terms)
    terms = [col_sums, lax.ppermute(col_sums, "col", [(i, i ^ 4) for i in range(col_count)])]
    other = lax.ppermute(other, "row", sibling)
    piece = (half, own, size, size)
    both, bias_sums = join(
        1.0 / math.sqrt(node_total), mine.reshape(piece), other.reshape(piece), terms
    )
    both = lax.all_to_all(both, "row", 0, 0, tiled=True, axis_index_groups=cores)
    grad_features, grad_weight = turn(both, own, weight)
    return activated, grad_features, grad_weight, bias_sums[0]


def solution(mesh):
    placed = (
        P(("row", "col"), None),
        P(),
        P(),
        P("row", "col", None, None, None),
        P("row", "col", None),
        P("row", "col", None),
        P("row", "col"),
        P(("row", "col"), None),
    )
    return jax.shard_map(
        on_device,
        mesh=mesh,
        in_specs=placed,
        out_specs=(P(("row", "col"), None), P(("row", "col"), None), P(), P()),
        check_vma=False,
    )
```

```python
import functools
import math

import jax
import jax.numpy as jnp
from jax import lax
from jax.experimental import pallas as pl
from jax.experimental.pallas import tpu as pltpu
from jax.sharding import PartitionSpec as P

f32 = jnp.float32
bf16 = jnp.bfloat16
STEP = 32
BIAS_ROWS = 8
RING = 4
VMEM_BYTES = 44 << 20
SMEM_SPEC = pl.BlockSpec(memory_space=pltpu.SMEM)
VMEM_SPEC = pl.BlockSpec(memory_space=pltpu.VMEM)
ANY_SPEC = pl.BlockSpec(memory_space=pl.ANY)


def nearness(ring, chip):
    return (ring + RING - chip // 2) % RING


def split(value):
    high = value.astype(bf16)
    return high, (value - high.astype(f32)).astype(bf16)


def tiles_kernel(flipped, starts, waits, count_ref, place_ref, pick_ref, *refs):
    pieces = refs[: len(starts)]
    refs = refs[len(starts) + waits :]
    adj_ref, *outs, total, tiles, source, tile_sem, piece_sem = refs
    out_blocks = sum(out.shape[0] for out in outs)
    size = adj_ref.shape[-1]
    count = count_ref[0]
    groups = (count + STEP - 1) // STEP

    def tile_copy(k):
        span = pl.ds(k * STEP, STEP)
        return pltpu.make_async_copy(adj_ref.at[span], tiles.at[span], tile_sem.at[k])

    def piece_copy(k):
        span = pl.ds(starts[k], pieces[k].shape[0])
        return pltpu.make_async_copy(pieces[k], source.at[span], piece_sem.at[k])

    for k in range(len(starts)):
        piece_copy(k).start()

    @pl.loop(0, groups)
    def _(k):
        tile_copy(k).start()

    @pl.loop(0, out_blocks + 1)
    def _(i):
        total[i] = jnp.zeros((size, size), f32)

    for k in range(len(starts)):
        piece_copy(k).wait()

    @pl.loop(0, groups)
    def _(k):
        tile_copy(k).wait()
        for u in range(STEP):
            slot = k * STEP + u
            place = jnp.where(slot < count, place_ref[slot], out_blocks)
            block = source[pick_ref[slot]]
            if flipped:
                product = jnp.dot(block, tiles[slot], preferred_element_type=f32)
            else:
                product = jnp.dot(tiles[slot], block, preferred_element_type=f32)
            total[place] += product

    filled = 0
    for out in outs:

        @pl.loop(0, out.shape[0] // 4)
        def _(i, out=out, filled=filled):
            out[pl.ds(i * 4, 4)] = total[pl.ds(filled + i * 4, 4)].astype(out.dtype)

        filled += out.shape[0]


def tile_products(count, place, pick, pieces, adj, outs, flipped, after=()):
    out_blocks = sum(outs)
    slots, size, _ = adj.shape
    starts, filled = [], 0
    for piece in pieces:
        starts.append(filled)
        filled += piece.shape[0]
    cost = pl.CostEstimate(
        flops=2 * slots * size**3, bytes_accessed=2 * slots * size**2, transcendentals=0
    )
    return pl.pallas_call(
        functools.partial(tiles_kernel, flipped, tuple(starts), len(after)),
        cost_estimate=cost,
        out_shape=tuple(jax.ShapeDtypeStruct((n, size, size), bf16) for n in outs),
        in_specs=[SMEM_SPEC] * 3 + [ANY_SPEC] * (len(pieces) + len(after) + 1),
        out_specs=(VMEM_SPEC,) * len(outs),
        scratch_shapes=[
            pltpu.VMEM((out_blocks + 1, size, size), f32),
            pltpu.VMEM((slots, size, size), bf16),
            pltpu.VMEM((filled, size, size), bf16),
            pltpu.SemaphoreType.DMA((slots // STEP,)),
            pltpu.SemaphoreType.DMA((len(pieces),)),
        ],
        compiler_params=pltpu.CompilerParams(vmem_limit_bytes=VMEM_BYTES),
        name="backward_tiles" if flipped else "forward_tiles",
    )(count, place, pick, *pieces, *after, adj)


def layer_kernel(me_ref, parts_ref, weight_ref, bias_ref, cot_ref, act_ref, turned_ref, grads_ref):
    aggregated = jnp.sum(parts_ref[...].astype(f32), axis=0)
    weight = weight_ref[...]
    high, low = split(aggregated)
    summed = jnp.dot(high, weight, preferred_element_type=f32)
    summed += jnp.dot(low, weight, preferred_element_type=f32)
    squashed = jnp.tanh(summed + bias_ref[...])
    act_ref[...] = squashed.astype(bf16)
    slopes = (cot_ref[...].astype(f32) * (1.0 - squashed * squashed)).astype(bf16)
    size = turned_ref.shape[-1]
    for i in range(turned_ref.shape[0]):
        rows = slopes[i * size : (i + 1) * size]
        turned_ref[i] = lax.dot_general(
            weight, rows, (((1,), (1,)), ((), ())), preferred_element_type=f32
        ).astype(bf16)
    high_t, low_t = split(aggregated.T)
    term = jnp.dot(high_t, slopes, preferred_element_type=f32)
    term += jnp.dot(low_t, slopes, preferred_element_type=f32)
    bias_term = jnp.sum(slopes.astype(f32), axis=0, keepdims=True)
    chunks, rows, width = grads_ref.shape
    held = rows - BIAS_ROWS
    for chunk in range(chunks):
        place = nearness(chunk, me_ref[0])
        grads_ref[place, :held] = term[chunk * held : (chunk + 1) * held]
        grads_ref[place, held:] = jnp.broadcast_to(bias_term, (BIAS_ROWS, width))


def layer(me, parts, weight, bias, cotangent, chips):
    nodes, units = cotangent.shape
    features = weight.shape[0]
    return pl.pallas_call(
        layer_kernel,
        out_shape=(
            jax.ShapeDtypeStruct((nodes, units), bf16),
            jax.ShapeDtypeStruct((nodes // 128, features, 128), bf16),
            jax.ShapeDtypeStruct((chips, features // chips + BIAS_ROWS, units), f32),
        ),
        in_specs=[SMEM_SPEC] + [VMEM_SPEC] * 4,
        out_specs=(VMEM_SPEC,) * 3,
        compiler_params=pltpu.CompilerParams(vmem_limit_bytes=VMEM_BYTES),
        name="layer",
    )(me, parts, weight, bias.reshape(1, units), cotangent)


def ring_sum_kernel(passing, *refs):
    own_ref, far_ref, up_ref, down_ref = refs[passing : passing + 4]
    kept = far_ref.shape[0]
    out_ref = refs[-1]
    out_ref[...] = (own_ref[:kept] + far_ref[...]) + (up_ref[...] + down_ref[...])


def ring_sum(passing, terms):
    count = len(passing)
    return pl.pallas_call(
        functools.partial(ring_sum_kernel, count),
        out_shape=tuple(jax.ShapeDtypeStruct(x.shape, x.dtype) for x in passing)
        + (jax.ShapeDtypeStruct(terms[1].shape, f32),),
        in_specs=[VMEM_SPEC] * count + [VMEM_SPEC] * 4,
        out_specs=(VMEM_SPEC,) * count + (VMEM_SPEC,),
        input_output_aliases={i: i for i in range(count)},
        compiler_params=pltpu.CompilerParams(vmem_limit_bytes=16 << 20),
        name="ring_sum",
    )(*passing, *terms)


def join_kernel(scale, mine_ref, other_ref, near_ref, far_ref, out_ref):
    pieces, blocks, size, _ = mine_ref.shape
    total = (near_ref[0] + far_ref[0]) * scale
    held = total.shape[0] - BIAS_ROWS
    high, low = split(total[held:])
    rows = lax.broadcasted_iota(jnp.int32, high.shape, 0)
    bias = jnp.where(rows < BIAS_ROWS // 2, high.astype(f32), low.astype(f32)).astype(bf16)
    both = jnp.concatenate([total[:held].astype(bf16), bias], axis=0)
    extra = jnp.concatenate([both[:, :size], both[:, size:]], axis=0)

    @pl.loop(0, pieces)
    def _(i):
        for b in range(blocks):
            both = mine_ref[i, b].astype(f32) + other_ref[i, b].astype(f32)
            out_ref[i, b * size : (b + 1) * size] = both.astype(bf16)
        out_ref[i, blocks * size :] = extra


def join(scale, mine, other, terms):
    pieces, blocks, size, _ = mine.shape
    _, rows, units = terms[0].shape
    extra = rows * units // size
    return pl.pallas_call(
        functools.partial(join_kernel, scale),
        out_shape=jax.ShapeDtypeStruct((pieces, blocks * size + extra, size), bf16),
        in_specs=[VMEM_SPEC] * 4,
        out_specs=VMEM_SPEC,
        compiler_params=pltpu.CompilerParams(vmem_limit_bytes=VMEM_BYTES),
        name="join",
    )(mine, other, *terms)


def turn_kernel(parts_ref, out_ref, grad_ref, bias_ref):
    pieces, rows, size = parts_ref.shape
    blocks = out_ref.shape[0] // size
    for i in range(blocks):
        total = jnp.sum(parts_ref[:, i * size : (i + 1) * size].astype(f32), axis=0)
        out_ref[i * size : (i + 1) * size, :] = total.T.astype(bf16)
    height = (rows - blocks * size) // 2
    held = height - BIAS_ROWS
    for side in range(2):
        lanes = slice(side * size, (side + 1) * size)
        first = blocks * size + side * height
        for p in range(0, pieces, 2):
            pair = parts_ref[p : p + 2, first : first + height].astype(f32)
            pair = pair[0] + pair[1]
            grad_ref[p // 2 * held : (p // 2 + 1) * held, lanes] = pair[:held]
            if p == 0:
                bias_ref[:, lanes] = pair[held : held + 1] + pair[held + 4 : held + 5]


def turn(parts, blocks, weight):
    size = parts.shape[-1]
    return pl.pallas_call(
        turn_kernel,
        out_shape=(
            jax.ShapeDtypeStruct((blocks * size, size), bf16),
            jax.ShapeDtypeStruct(weight.shape, f32),
            jax.ShapeDtypeStruct((1, weight.shape[1]), f32),
        ),
        in_specs=[VMEM_SPEC],
        out_specs=(VMEM_SPEC,) * 3,
        compiler_params=pltpu.CompilerParams(vmem_limit_bytes=VMEM_BYTES),
        name="turn",
    )(parts)


def on_device(
    features, weight, layer_bias, adj_tiles, tile_rows, tile_cols, tile_counts, cotangent
):
    row_count = lax.axis_size("row")
    col_count = lax.axis_size("col")
    size = adj_tiles.shape[-1]
    own = features.shape[0] // size
    row_blocks = own * col_count
    col_blocks = own * row_count
    half = row_count // 2
    node_total = features.shape[0] * row_count * col_count
    adj = adj_tiles[0, 0]
    rows = tile_rows[0, 0]
    cols = tile_cols[0, 0]
    count = tile_counts[0]
    my_row = lax.axis_index("row")
    my_col = lax.axis_index("col")
    chip = (my_row // 2).reshape(1)
    cores = [[2 * k + c for k in range(half)] for c in range(2)]
    sibling = [(i, i ^ 1) for i in range(row_count)]

    mine = features.reshape(1, own, size, -1)
    mine = lax.all_to_all(
        jnp.broadcast_to(mine, (half,) + mine.shape[1:]),
        "row", 0, 0, tiled=True, axis_index_groups=cores,
    ).reshape(half * own, size, -1)
    other = lax.ppermute(mine, "row", sibling)
    owner = cols // own
    cols_slot = ((owner ^ my_row) & 1) * (half * own) + (owner // 2) * own + cols % own
    (partial_value,) = tile_products(count, rows, cols_slot, [mine, other], adj, [row_blocks], False)
    parts = lax.all_to_all(
        partial_value.reshape(col_count, own * size, -1), "col", 0, 0, tiled=True
    )
    activated, turned, grads = layer(chip, parts, weight, layer_bias, cotangent, RING)

    pair = lax.ppermute(turned, "col", [(i, i ^ 4) for i in range(col_count)])
    up = [(i, (i // 4) * 4 + (i + 1) % 4) for i in range(col_count)]
    down = [(i, (i // 4) * 4 + (i + 3) % 4) for i in range(col_count)]
    block = jnp.concatenate([turned, pair], axis=0)
    before = lax.ppermute(block, "col", up)
    after = lax.ppermute(block, "col", down)
    far_top = lax.ppermute(before[:own], "col", up)
    far_low = lax.ppermute(after[own:], "col", down)
    pieces = [block, after, far_top, far_low, before]
    owner = rows // own
    far = ((owner - my_col) % 4) * 2 + (owner ^ my_col) // 4
    rows_slot = far * own + rows % own
    grads += lax.ppermute(grads, "row", sibling)
    y_up = [(i, (i + 4) % row_count) for i in range(row_count)]
    y_down = [(i, (i - 4) % row_count) for i in range(row_count)]
    y_far = [(i, (i + 8) % row_count) for i in range(row_count)]
    row_sums = (grads[:1] + lax.ppermute(grads[2:3], "row", y_far)) + (
        lax.ppermute(grads[1:2], "row", y_up) + lax.ppermute(grads[3:], "row", y_down)
    )
    x_far = [(i, (i // 4) * 4 + (i + 2) % 4) for i in range(col_count)]
    terms = [row_sums] + [lax.ppermute(row_sums, "col", to) for to in (x_far, up, down)]

    mine, other = tile_products(count, cols_slot, rows_slot, pieces, adj, [col_blocks // 2] * 2, True, [row_sums])
    other, col_sums = ring_sum([other], terms)
    terms = [col_sums, lax.ppermute(col_sums, "col", [(i, i ^ 4) for i in range(col_count)])]
    other = lax.ppermute(other, "row", sibling)
    piece = (half, own, size, size)
    both = join(
        1.0 / math.sqrt(node_total), mine.reshape(piece), other.reshape(piece), terms
    )
    both = lax.all_to_all(both, "row", 0, 0, tiled=True, axis_index_groups=cores)
    grad_features, grad_weight, grad_bias = turn(both, own, weight)
    return activated, grad_features, grad_weight, grad_bias[0]


def solution(mesh):
    placed = (
        P(("row", "col"), None),
        P(),
        P(),
        P("row", "col", None, None, None),
        P("row", "col", None),
        P("row", "col", None),
        P("row", "col"),
        P(("row", "col"), None),
    )
    return jax.shard_map(
        on_device,
        mesh=mesh,
        in_specs=placed,
        out_specs=(P(("row", "col"), None), P(("row", "col"), None), P(), P()),
        check_vma=False,
    )
```

```python
import functools
import math

import jax
import jax.numpy as jnp
from jax import lax
from jax.experimental import pallas as pl
from jax.experimental.pallas import tpu as pltpu
from jax.sharding import PartitionSpec as P

f32 = jnp.float32
bf16 = jnp.bfloat16
STEP = 32
BIAS_ROWS = 8
RING = 4
VMEM_BYTES = 44 << 20
SMEM_SPEC = pl.BlockSpec(memory_space=pltpu.SMEM)
VMEM_SPEC = pl.BlockSpec(memory_space=pltpu.VMEM)
ANY_SPEC = pl.BlockSpec(memory_space=pl.ANY)


def nearness(ring, chip):
    return (ring + RING - chip // 2) % RING


def split(value):
    high = value.astype(bf16)
    return high, (value - high.astype(f32)).astype(bf16)


def tiles_kernel(flipped, starts, waits, count_ref, place_ref, pick_ref, *refs):
    pieces = refs[: len(starts)]
    refs = refs[len(starts) + waits :]
    adj_ref, *outs, total, tiles, source, tile_sem, piece_sem = refs
    out_blocks = sum(out.shape[0] for out in outs)
    size = adj_ref.shape[-1]
    count = count_ref[0]
    groups = (count + STEP - 1) // STEP

    def tile_copy(k):
        span = pl.ds(k * STEP, STEP)
        return pltpu.make_async_copy(adj_ref.at[span], tiles.at[span], tile_sem.at[k])

    def piece_copy(k):
        span = pl.ds(starts[k], pieces[k].shape[0])
        return pltpu.make_async_copy(pieces[k], source.at[span], piece_sem.at[k])

    for k in range(len(starts)):
        piece_copy(k).start()

    @pl.loop(0, groups)
    def _(k):
        tile_copy(k).start()

    @pl.loop(0, out_blocks + 1)
    def _(i):
        total[i] = jnp.zeros((size, size), f32)

    for k in range(len(starts)):
        piece_copy(k).wait()

    @pl.loop(0, groups)
    def _(k):
        tile_copy(k).wait()
        for u in range(STEP):
            slot = k * STEP + u
            place = jnp.where(slot < count, place_ref[slot], out_blocks)
            block = source[pick_ref[slot]]
            if flipped:
                product = jnp.dot(block, tiles[slot], preferred_element_type=f32)
            else:
                product = jnp.dot(tiles[slot], block, preferred_element_type=f32)
            total[place] += product

    filled = 0
    for out in outs:

        @pl.loop(0, out.shape[0] // 4)
        def _(i, out=out, filled=filled):
            out[pl.ds(i * 4, 4)] = total[pl.ds(filled + i * 4, 4)].astype(out.dtype)

        filled += out.shape[0]


def tile_products(count, place, pick, pieces, adj, outs, flipped, after=()):
    out_blocks = sum(outs)
    slots, size, _ = adj.shape
    starts, filled = [], 0
    for piece in pieces:
        starts.append(filled)
        filled += piece.shape[0]
    cost = pl.CostEstimate(
        flops=2 * slots * size**3, bytes_accessed=2 * slots * size**2, transcendentals=0
    )
    return pl.pallas_call(
        functools.partial(tiles_kernel, flipped, tuple(starts), len(after)),
        cost_estimate=cost,
        out_shape=tuple(jax.ShapeDtypeStruct((n, size, size), bf16) for n in outs),
        in_specs=[SMEM_SPEC] * 3 + [ANY_SPEC] * (len(pieces) + len(after) + 1),
        out_specs=(VMEM_SPEC,) * len(outs),
        scratch_shapes=[
            pltpu.VMEM((out_blocks + 1, size, size), f32),
            pltpu.VMEM((slots, size, size), bf16),
            pltpu.VMEM((filled, size, size), bf16),
            pltpu.SemaphoreType.DMA((slots // STEP,)),
            pltpu.SemaphoreType.DMA((len(pieces),)),
        ],
        compiler_params=pltpu.CompilerParams(vmem_limit_bytes=VMEM_BYTES),
        name="backward_tiles" if flipped else "forward_tiles",
    )(count, place, pick, *pieces, *after, adj)


def layer_kernel(
    parts_ref, weight_ref, bias_ref, cot_ref, act_ref, turned_ref, agg_ref, slopes_ref
):
    aggregated = jnp.sum(parts_ref[...].astype(f32), axis=0)
    weight = weight_ref[...]
    high, low = split(aggregated)
    summed = jnp.dot(high, weight, preferred_element_type=f32)
    summed += jnp.dot(low, weight, preferred_element_type=f32)
    squashed = jnp.tanh(summed + bias_ref[...])
    act_ref[...] = squashed.astype(bf16)
    slopes = (cot_ref[...].astype(f32) * (1.0 - squashed * squashed)).astype(bf16)
    size = turned_ref.shape[-1]
    for i in range(turned_ref.shape[0]):
        rows = slopes[i * size : (i + 1) * size]
        turned_ref[i] = lax.dot_general(
            weight, rows, (((1,), (1,)), ((), ())), preferred_element_type=f32
        ).astype(bf16)
    agg_ref[...] = aggregated
    slopes_ref[...] = slopes


def weight_kernel(me_ref, agg_ref, slopes_ref, grads_ref):
    slopes = slopes_ref[...]
    high_t, low_t = split(agg_ref[...].T)
    term = jnp.dot(high_t, slopes, preferred_element_type=f32)
    term += jnp.dot(low_t, slopes, preferred_element_type=f32)
    bias_term = jnp.sum(slopes.astype(f32), axis=0, keepdims=True)
    chunks, rows, width = grads_ref.shape
    held = rows - BIAS_ROWS
    for chunk in range(chunks):
        place = nearness(chunk, me_ref[0])
        grads_ref[place, :held] = term[chunk * held : (chunk + 1) * held]
        grads_ref[place, held:] = jnp.broadcast_to(bias_term, (BIAS_ROWS, width))


def layer(parts, weight, bias, cotangent):
    nodes, units = cotangent.shape
    features = weight.shape[0]
    return pl.pallas_call(
        layer_kernel,
        out_shape=(
            jax.ShapeDtypeStruct((nodes, units), bf16),
            jax.ShapeDtypeStruct((nodes // 128, features, 128), bf16),
            jax.ShapeDtypeStruct((nodes, features), f32),
            jax.ShapeDtypeStruct((nodes, units), bf16),
        ),
        in_specs=[VMEM_SPEC] * 4,
        out_specs=(VMEM_SPEC,) * 4,
        compiler_params=pltpu.CompilerParams(vmem_limit_bytes=VMEM_BYTES),
        name="layer",
    )(parts, weight, bias.reshape(1, units), cotangent)


def weight_terms(me, aggregated, slopes, chips):
    features, units = aggregated.shape[1], slopes.shape[1]
    return pl.pallas_call(
        weight_kernel,
        out_shape=jax.ShapeDtypeStruct((chips, features // chips + BIAS_ROWS, units), f32),
        in_specs=[SMEM_SPEC] + [VMEM_SPEC] * 2,
        out_specs=VMEM_SPEC,
        compiler_params=pltpu.CompilerParams(vmem_limit_bytes=VMEM_BYTES),
        name="weight_terms",
    )(me, aggregated, slopes)


def ring_sum_kernel(passing, *refs):
    own_ref, far_ref, up_ref, down_ref = refs[passing : passing + 4]
    kept = far_ref.shape[0]
    out_ref = refs[-1]
    out_ref[...] = (own_ref[:kept] + far_ref[...]) + (up_ref[...] + down_ref[...])


def ring_sum(passing, terms):
    count = len(passing)
    return pl.pallas_call(
        functools.partial(ring_sum_kernel, count),
        out_shape=tuple(jax.ShapeDtypeStruct(x.shape, x.dtype) for x in passing)
        + (jax.ShapeDtypeStruct(terms[1].shape, f32),),
        in_specs=[VMEM_SPEC] * count + [VMEM_SPEC] * 4,
        out_specs=(VMEM_SPEC,) * count + (VMEM_SPEC,),
        input_output_aliases={i: i for i in range(count)},
        compiler_params=pltpu.CompilerParams(vmem_limit_bytes=16 << 20),
        name="ring_sum",
    )(*passing, *terms)


def join_kernel(scale, mine_ref, other_ref, near_ref, far_ref, out_ref):
    pieces, blocks, size, _ = mine_ref.shape
    total = (near_ref[0] + far_ref[0]) * scale
    held = total.shape[0] - BIAS_ROWS
    high, low = split(total[held:])
    rows = lax.broadcasted_iota(jnp.int32, high.shape, 0)
    bias = jnp.where(rows < BIAS_ROWS // 2, high.astype(f32), low.astype(f32)).astype(bf16)
    both = jnp.concatenate([total[:held].astype(bf16), bias], axis=0)
    extra = jnp.concatenate([both[:, :size], both[:, size:]], axis=0)

    @pl.loop(0, pieces)
    def _(i):
        for b in range(blocks):
            both = mine_ref[i, b].astype(f32) + other_ref[i, b].astype(f32)
            out_ref[i, b * size : (b + 1) * size] = both.astype(bf16)
        out_ref[i, blocks * size :] = extra


def join(scale, mine, other, terms):
    pieces, blocks, size, _ = mine.shape
    _, rows, units = terms[0].shape
    extra = rows * units // size
    return pl.pallas_call(
        functools.partial(join_kernel, scale),
        out_shape=jax.ShapeDtypeStruct((pieces, blocks * size + extra, size), bf16),
        in_specs=[VMEM_SPEC] * 4,
        out_specs=VMEM_SPEC,
        compiler_params=pltpu.CompilerParams(vmem_limit_bytes=VMEM_BYTES),
        name="join",
    )(mine, other, *terms)


def turn_kernel(parts_ref, out_ref, grad_ref, bias_ref):
    pieces, rows, size = parts_ref.shape
    blocks = out_ref.shape[0] // size
    for i in range(blocks):
        total = jnp.sum(parts_ref[:, i * size : (i + 1) * size].astype(f32), axis=0)
        out_ref[i * size : (i + 1) * size, :] = total.T.astype(bf16)
    height = (rows - blocks * size) // 2
    held = height - BIAS_ROWS
    for side in range(2):
        lanes = slice(side * size, (side + 1) * size)
        first = blocks * size + side * height
        for p in range(0, pieces, 2):
            pair = parts_ref[p : p + 2, first : first + height].astype(f32)
            pair = pair[0] + pair[1]
            grad_ref[p // 2 * held : (p // 2 + 1) * held, lanes] = pair[:held]
            if p == 0:
                bias_ref[:, lanes] = pair[held : held + 1] + pair[held + 4 : held + 5]


def turn(parts, blocks, weight):
    size = parts.shape[-1]
    return pl.pallas_call(
        turn_kernel,
        out_shape=(
            jax.ShapeDtypeStruct((blocks * size, size), bf16),
            jax.ShapeDtypeStruct(weight.shape, f32),
            jax.ShapeDtypeStruct((1, weight.shape[1]), f32),
        ),
        in_specs=[VMEM_SPEC],
        out_specs=(VMEM_SPEC,) * 3,
        compiler_params=pltpu.CompilerParams(vmem_limit_bytes=VMEM_BYTES),
        name="turn",
    )(parts)


def on_device(
    features, weight, layer_bias, adj_tiles, tile_rows, tile_cols, tile_counts, cotangent
):
    row_count = lax.axis_size("row")
    col_count = lax.axis_size("col")
    size = adj_tiles.shape[-1]
    own = features.shape[0] // size
    row_blocks = own * col_count
    col_blocks = own * row_count
    half = row_count // 2
    node_total = features.shape[0] * row_count * col_count
    adj = adj_tiles[0, 0]
    rows = tile_rows[0, 0]
    cols = tile_cols[0, 0]
    count = tile_counts[0]
    my_row = lax.axis_index("row")
    my_col = lax.axis_index("col")
    chip = (my_row // 2).reshape(1)
    cores = [[2 * k + c for k in range(half)] for c in range(2)]
    sibling = [(i, i ^ 1) for i in range(row_count)]

    mine = features.reshape(1, own, size, -1)
    mine = lax.all_to_all(
        jnp.broadcast_to(mine, (half,) + mine.shape[1:]),
        "row", 0, 0, tiled=True, axis_index_groups=cores,
    ).reshape(half * own, size, -1)
    other = lax.ppermute(mine, "row", sibling)
    owner = cols // own
    cols_slot = ((owner ^ my_row) & 1) * (half * own) + (owner // 2) * own + cols % own
    (partial_value,) = tile_products(count, rows, cols_slot, [mine, other], adj, [row_blocks], False)
    parts = lax.all_to_all(
        partial_value.reshape(col_count, own * size, -1), "col", 0, 0, tiled=True
    )
    activated, turned, aggregated, slopes = layer(parts, weight, layer_bias, cotangent)
    grads = weight_terms(chip, aggregated, slopes, RING)

    pair = lax.ppermute(turned, "col", [(i, i ^ 4) for i in range(col_count)])
    up = [(i, (i // 4) * 4 + (i + 1) % 4) for i in range(col_count)]
    down = [(i, (i // 4) * 4 + (i + 3) % 4) for i in range(col_count)]
    block = jnp.concatenate([turned, pair], axis=0)
    before = lax.ppermute(block, "col", up)
    after = lax.ppermute(block, "col", down)
    far_top = lax.ppermute(before[:own], "col", up)
    far_low = lax.ppermute(after[own:], "col", down)
    pieces = [block, after, far_top, far_low, before]
    owner = rows // own
    far = ((owner - my_col) % 4) * 2 + (owner ^ my_col) // 4
    rows_slot = far * own + rows % own
    grads += lax.ppermute(grads, "row", sibling)
    y_up = [(i, (i + 4) % row_count) for i in range(row_count)]
    y_down = [(i, (i - 4) % row_count) for i in range(row_count)]
    y_far = [(i, (i + 8) % row_count) for i in range(row_count)]
    row_sums = (grads[:1] + lax.ppermute(grads[2:3], "row", y_far)) + (
        lax.ppermute(grads[1:2], "row", y_up) + lax.ppermute(grads[3:], "row", y_down)
    )
    x_far = [(i, (i // 4) * 4 + (i + 2) % 4) for i in range(col_count)]
    terms = [row_sums] + [lax.ppermute(row_sums, "col", to) for to in (x_far, up, down)]

    mine, other = tile_products(count, cols_slot, rows_slot, pieces, adj, [col_blocks // 2] * 2, True, [row_sums])
    other, col_sums = ring_sum([other], terms)
    terms = [col_sums, lax.ppermute(col_sums, "col", [(i, i ^ 4) for i in range(col_count)])]
    other = lax.ppermute(other, "row", sibling)
    piece = (half, own, size, size)
    both = join(
        1.0 / math.sqrt(node_total), mine.reshape(piece), other.reshape(piece), terms
    )
    both = lax.all_to_all(both, "row", 0, 0, tiled=True, axis_index_groups=cores)
    grad_features, grad_weight, grad_bias = turn(both, own, weight)
    return activated, grad_features, grad_weight, grad_bias[0]


def solution(mesh):
    placed = (
        P(("row", "col"), None),
        P(),
        P(),
        P("row", "col", None, None, None),
        P("row", "col", None),
        P("row", "col", None),
        P("row", "col"),
        P(("row", "col"), None),
    )
    return jax.shard_map(
        on_device,
        mesh=mesh,
        in_specs=placed,
        out_specs=(P(("row", "col"), None), P(("row", "col"), None), P(), P()),
        check_vma=False,
    )
```

```python
import functools
import math

import jax
import jax.numpy as jnp
from jax import lax
from jax.experimental import pallas as pl
from jax.experimental.pallas import tpu as pltpu
from jax.sharding import PartitionSpec as P

f32 = jnp.float32
bf16 = jnp.bfloat16
STEP = 48
BIAS_ROWS = 8
RING = 4
VMEM_BYTES = 44 << 20
SMEM_SPEC = pl.BlockSpec(memory_space=pltpu.SMEM)
VMEM_SPEC = pl.BlockSpec(memory_space=pltpu.VMEM)
ANY_SPEC = pl.BlockSpec(memory_space=pl.ANY)


def nearness(ring, chip):
    return (ring + RING - chip // 2) % RING


def split(value):
    high = value.astype(bf16)
    return high, (value - high.astype(f32)).astype(bf16)


def tiles_kernel(flipped, starts, waits, count_ref, place_ref, pick_ref, *refs):
    pieces = refs[: len(starts)]
    refs = refs[len(starts) + waits :]
    adj_ref, *outs, total, tiles, source, tile_sem, piece_sem = refs
    out_blocks = sum(out.shape[0] for out in outs)
    size = adj_ref.shape[-1]
    count = count_ref[0]
    groups = (count + STEP - 1) // STEP

    def tile_copy(k):
        span = pl.ds(k * STEP, STEP)
        return pltpu.make_async_copy(adj_ref.at[span], tiles.at[span], tile_sem.at[k])

    def piece_copy(k):
        span = pl.ds(starts[k], pieces[k].shape[0])
        return pltpu.make_async_copy(pieces[k], source.at[span], piece_sem.at[k])

    for k in range(len(starts)):
        piece_copy(k).start()

    @pl.loop(0, groups)
    def _(k):
        tile_copy(k).start()

    @pl.loop(0, out_blocks + 1)
    def _(i):
        total[i] = jnp.zeros((size, size), f32)

    for k in range(len(starts)):
        piece_copy(k).wait()

    @pl.loop(0, groups)
    def _(k):
        tile_copy(k).wait()
        for u in range(STEP):
            slot = k * STEP + u
            place = jnp.where(slot < count, place_ref[slot], out_blocks)
            block = source[pick_ref[slot]]
            if flipped:
                product = jnp.dot(block, tiles[slot], preferred_element_type=f32)
            else:
                product = jnp.dot(tiles[slot], block, preferred_element_type=f32)
            total[place] += product

    filled = 0
    for out in outs:

        @pl.loop(0, out.shape[0] // 4)
        def _(i, out=out, filled=filled):
            out[pl.ds(i * 4, 4)] = total[pl.ds(filled + i * 4, 4)].astype(out.dtype)

        filled += out.shape[0]


def tile_products(count, place, pick, pieces, adj, outs, flipped, after=()):
    out_blocks = sum(outs)
    slots, size, _ = adj.shape
    starts, filled = [], 0
    for piece in pieces:
        starts.append(filled)
        filled += piece.shape[0]
    cost = pl.CostEstimate(
        flops=2 * slots * size**3, bytes_accessed=2 * slots * size**2, transcendentals=0
    )
    return pl.pallas_call(
        functools.partial(tiles_kernel, flipped, tuple(starts), len(after)),
        cost_estimate=cost,
        out_shape=tuple(jax.ShapeDtypeStruct((n, size, size), bf16) for n in outs),
        in_specs=[SMEM_SPEC] * 3 + [ANY_SPEC] * (len(pieces) + len(after) + 1),
        out_specs=(VMEM_SPEC,) * len(outs),
        scratch_shapes=[
            pltpu.VMEM((out_blocks + 1, size, size), f32),
            pltpu.VMEM((slots, size, size), bf16),
            pltpu.VMEM((filled, size, size), bf16),
            pltpu.SemaphoreType.DMA((slots // STEP,)),
            pltpu.SemaphoreType.DMA((len(pieces),)),
        ],
        compiler_params=pltpu.CompilerParams(vmem_limit_bytes=VMEM_BYTES),
        name="backward_tiles" if flipped else "forward_tiles",
    )(count, place, pick, *pieces, *after, adj)


def layer_kernel(
    parts_ref, weight_ref, bias_ref, cot_ref, act_ref, turned_ref, agg_ref, slopes_ref
):
    aggregated = jnp.sum(parts_ref[...].astype(f32), axis=0)
    weight = weight_ref[...]
    high, low = split(aggregated)
    summed = jnp.dot(high, weight, preferred_element_type=f32)
    summed += jnp.dot(low, weight, preferred_element_type=f32)
    squashed = jnp.tanh(summed + bias_ref[...])
    act_ref[...] = squashed.astype(bf16)
    slopes = (cot_ref[...].astype(f32) * (1.0 - squashed * squashed)).astype(bf16)
    size = turned_ref.shape[-1]
    for i in range(turned_ref.shape[0]):
        rows = slopes[i * size : (i + 1) * size]
        turned_ref[i] = lax.dot_general(
            weight, rows, (((1,), (1,)), ((), ())), preferred_element_type=f32
        ).astype(bf16)
    agg_ref[...] = aggregated
    slopes_ref[...] = slopes


def weight_kernel(me_ref, agg_ref, slopes_ref, grads_ref):
    slopes = slopes_ref[...]
    high_t, low_t = split(agg_ref[...].T)
    term = jnp.dot(high_t, slopes, preferred_element_type=f32)
    term += jnp.dot(low_t, slopes, preferred_element_type=f32)
    bias_term = jnp.sum(slopes.astype(f32), axis=0, keepdims=True)
    chunks, rows, width = grads_ref.shape
    held = rows - BIAS_ROWS
    for chunk in range(chunks):
        place = nearness(chunk, me_ref[0])
        grads_ref[place, :held] = term[chunk * held : (chunk + 1) * held]
        grads_ref[place, held:] = jnp.broadcast_to(bias_term, (BIAS_ROWS, width))


def layer(parts, weight, bias, cotangent):
    nodes, units = cotangent.shape
    features = weight.shape[0]
    return pl.pallas_call(
        layer_kernel,
        out_shape=(
            jax.ShapeDtypeStruct((nodes, units), bf16),
            jax.ShapeDtypeStruct((nodes // 128, features, 128), bf16),
            jax.ShapeDtypeStruct((nodes, features), f32),
            jax.ShapeDtypeStruct((nodes, units), bf16),
        ),
        in_specs=[VMEM_SPEC] * 4,
        out_specs=(VMEM_SPEC,) * 4,
        compiler_params=pltpu.CompilerParams(vmem_limit_bytes=VMEM_BYTES),
        name="layer",
    )(parts, weight, bias.reshape(1, units), cotangent)


def weight_terms(me, aggregated, slopes, chips):
    features, units = aggregated.shape[1], slopes.shape[1]
    return pl.pallas_call(
        weight_kernel,
        out_shape=jax.ShapeDtypeStruct((chips, features // chips + BIAS_ROWS, units), f32),
        in_specs=[SMEM_SPEC] + [VMEM_SPEC] * 2,
        out_specs=VMEM_SPEC,
        compiler_params=pltpu.CompilerParams(vmem_limit_bytes=VMEM_BYTES),
        name="weight_terms",
    )(me, aggregated, slopes)


def ring_sum_kernel(passing, *refs):
    own_ref, far_ref, up_ref, down_ref = refs[passing : passing + 4]
    kept = far_ref.shape[0]
    out_ref = refs[-1]
    out_ref[...] = (own_ref[:kept] + far_ref[...]) + (up_ref[...] + down_ref[...])


def ring_sum(passing, terms):
    count = len(passing)
    return pl.pallas_call(
        functools.partial(ring_sum_kernel, count),
        out_shape=tuple(jax.ShapeDtypeStruct(x.shape, x.dtype) for x in passing)
        + (jax.ShapeDtypeStruct(terms[1].shape, f32),),
        in_specs=[VMEM_SPEC] * count + [VMEM_SPEC] * 4,
        out_specs=(VMEM_SPEC,) * count + (VMEM_SPEC,),
        input_output_aliases={i: i for i in range(count)},
        compiler_params=pltpu.CompilerParams(vmem_limit_bytes=16 << 20),
        name="ring_sum",
    )(*passing, *terms)


def join_kernel(scale, mine_ref, other_ref, near_ref, far_ref, out_ref):
    pieces, blocks, size, _ = mine_ref.shape
    total = (near_ref[0] + far_ref[0]) * scale
    held = total.shape[0] - BIAS_ROWS
    high, low = split(total[held:])
    rows = lax.broadcasted_iota(jnp.int32, high.shape, 0)
    bias = jnp.where(rows < BIAS_ROWS // 2, high.astype(f32), low.astype(f32)).astype(bf16)
    both = jnp.concatenate([total[:held].astype(bf16), bias], axis=0)
    extra = jnp.concatenate([both[:, :size], both[:, size:]], axis=0)

    @pl.loop(0, pieces)
    def _(i):
        for b in range(blocks):
            both = mine_ref[i, b].astype(f32) + other_ref[i, b].astype(f32)
            out_ref[i, b * size : (b + 1) * size] = both.astype(bf16)
        out_ref[i, blocks * size :] = extra


def join(scale, mine, other, terms):
    pieces, blocks, size, _ = mine.shape
    _, rows, units = terms[0].shape
    extra = rows * units // size
    return pl.pallas_call(
        functools.partial(join_kernel, scale),
        out_shape=jax.ShapeDtypeStruct((pieces, blocks * size + extra, size), bf16),
        in_specs=[VMEM_SPEC] * 4,
        out_specs=VMEM_SPEC,
        compiler_params=pltpu.CompilerParams(vmem_limit_bytes=VMEM_BYTES),
        name="join",
    )(mine, other, *terms)


def turn_kernel(parts_ref, out_ref, grad_ref, bias_ref):
    pieces, rows, size = parts_ref.shape
    blocks = out_ref.shape[0] // size
    for i in range(blocks):
        total = jnp.sum(parts_ref[:, i * size : (i + 1) * size].astype(f32), axis=0)
        out_ref[i * size : (i + 1) * size, :] = total.T.astype(bf16)
    height = (rows - blocks * size) // 2
    held = height - BIAS_ROWS
    for side in range(2):
        lanes = slice(side * size, (side + 1) * size)
        first = blocks * size + side * height
        for p in range(0, pieces, 2):
            pair = parts_ref[p : p + 2, first : first + height].astype(f32)
            pair = pair[0] + pair[1]
            grad_ref[p // 2 * held : (p // 2 + 1) * held, lanes] = pair[:held]
            if p == 0:
                bias_ref[:, lanes] = pair[held : held + 1] + pair[held + 4 : held + 5]


def turn(parts, blocks, weight):
    size = parts.shape[-1]
    return pl.pallas_call(
        turn_kernel,
        out_shape=(
            jax.ShapeDtypeStruct((blocks * size, size), bf16),
            jax.ShapeDtypeStruct(weight.shape, f32),
            jax.ShapeDtypeStruct((1, weight.shape[1]), f32),
        ),
        in_specs=[VMEM_SPEC],
        out_specs=(VMEM_SPEC,) * 3,
        compiler_params=pltpu.CompilerParams(vmem_limit_bytes=VMEM_BYTES),
        name="turn",
    )(parts)


def on_device(
    features, weight, layer_bias, adj_tiles, tile_rows, tile_cols, tile_counts, cotangent
):
    row_count = lax.axis_size("row")
    col_count = lax.axis_size("col")
    size = adj_tiles.shape[-1]
    own = features.shape[0] // size
    row_blocks = own * col_count
    col_blocks = own * row_count
    half = row_count // 2
    node_total = features.shape[0] * row_count * col_count
    adj = adj_tiles[0, 0]
    rows = tile_rows[0, 0]
    cols = tile_cols[0, 0]
    count = tile_counts[0]
    my_row = lax.axis_index("row")
    my_col = lax.axis_index("col")
    chip = (my_row // 2).reshape(1)
    cores = [[2 * k + c for k in range(half)] for c in range(2)]
    sibling = [(i, i ^ 1) for i in range(row_count)]

    mine = features.reshape(1, own, size, -1)
    mine = lax.all_to_all(
        jnp.broadcast_to(mine, (half,) + mine.shape[1:]),
        "row", 0, 0, tiled=True, axis_index_groups=cores,
    ).reshape(half * own, size, -1)
    other = lax.ppermute(mine, "row", sibling)
    owner = cols // own
    cols_slot = ((owner ^ my_row) & 1) * (half * own) + (owner // 2) * own + cols % own
    (partial_value,) = tile_products(count, rows, cols_slot, [mine, other], adj, [row_blocks], False)
    parts = lax.all_to_all(
        partial_value.reshape(col_count, own * size, -1), "col", 0, 0, tiled=True
    )
    activated, turned, aggregated, slopes = layer(parts, weight, layer_bias, cotangent)
    grads = weight_terms(chip, aggregated, slopes, RING)

    pair = lax.ppermute(turned, "col", [(i, i ^ 4) for i in range(col_count)])
    up = [(i, (i // 4) * 4 + (i + 1) % 4) for i in range(col_count)]
    down = [(i, (i // 4) * 4 + (i + 3) % 4) for i in range(col_count)]
    block = jnp.concatenate([turned, pair], axis=0)
    before = lax.ppermute(block, "col", up)
    after = lax.ppermute(block, "col", down)
    far_top = lax.ppermute(before[:own], "col", up)
    far_low = lax.ppermute(after[own:], "col", down)
    pieces = [block, after, far_top, far_low, before]
    owner = rows // own
    far = ((owner - my_col) % 4) * 2 + (owner ^ my_col) // 4
    rows_slot = far * own + rows % own
    grads += lax.ppermute(grads, "row", sibling)
    y_up = [(i, (i + 4) % row_count) for i in range(row_count)]
    y_down = [(i, (i - 4) % row_count) for i in range(row_count)]
    y_far = [(i, (i + 8) % row_count) for i in range(row_count)]
    row_sums = (grads[:1] + lax.ppermute(grads[2:3], "row", y_far)) + (
        lax.ppermute(grads[1:2], "row", y_up) + lax.ppermute(grads[3:], "row", y_down)
    )
    x_far = [(i, (i // 4) * 4 + (i + 2) % 4) for i in range(col_count)]
    terms = [row_sums] + [lax.ppermute(row_sums, "col", to) for to in (x_far, up, down)]

    mine, other = tile_products(count, cols_slot, rows_slot, pieces, adj, [col_blocks // 2] * 2, True, [row_sums])
    other, col_sums = ring_sum([other], terms)
    terms = [col_sums, lax.ppermute(col_sums, "col", [(i, i ^ 4) for i in range(col_count)])]
    other = lax.ppermute(other, "row", sibling)
    piece = (half, own, size, size)
    both = join(
        1.0 / math.sqrt(node_total), mine.reshape(piece), other.reshape(piece), terms
    )
    both = lax.all_to_all(both, "row", 0, 0, tiled=True, axis_index_groups=cores)
    grad_features, grad_weight, grad_bias = turn(both, own, weight)
    return activated, grad_features, grad_weight, grad_bias[0]


def solution(mesh):
    placed = (
        P(("row", "col"), None),
        P(),
        P(),
        P("row", "col", None, None, None),
        P("row", "col", None),
        P("row", "col", None),
        P("row", "col"),
        P(("row", "col"), None),
    )
    return jax.shard_map(
        on_device,
        mesh=mesh,
        in_specs=placed,
        out_specs=(P(("row", "col"), None), P(("row", "col"), None), P(), P()),
        check_vma=False,
    )
```
